32 devices in a mesh: layer: 2 (over x), row: 4 (over z), col: 4 (over y, core).
Axes of the slice: x: 2, y: 2, z: 4, core: 2. Of those that a mesh axis runs over, the one named last changes fastest.
Arguments:
- rhs_root: float32 [16384, 128], P('col'), may hold values from -6 to 6
- rhs_child: float32 [2, 8192, 128], P('layer', 'col'), may hold values from -6 to 6
- rhs_leaf: float32 [4, 4096, 128], P('layer', 'col'), may hold values from -6 to 6
- root_inv: bfloat16 [16384, 16384], P('row', 'col'), may hold values from -0.046875 to 0.046875
- child_inv: bfloat16 [2, 8192, 8192], P('layer', 'row', 'col'), may hold values from -0.0625 to 0.0625
- leaf_inv: bfloat16 [4, 4096, 4096], P('layer', 'row', 'col'), may hold values from -0.09375 to 0.09375
- leaf_to_child: bfloat16 [4, 8192, 4096], P('layer', 'col', 'row'), may hold values from -0.0625 to 0.0625
- leaf_to_root: bfloat16 [4, 16384, 4096], P('layer', 'col', 'row'), may hold values from -0.03125 to 0.03125
- child_to_root: bfloat16 [2, 16384, 8192], P('layer', 'col', 'row'), may hold values from -0.03125 to 0.03125
Outputs:
- x_root: float32 [16384, 128], P('col')
- x_child: float32 [2, 8192, 128], P('layer', 'col')
- x_leaf: float32 [4, 4096, 128], P('layer', 'col')
- y_root: float32 [16384, 128], P('row')
The draws below stay inside these ranges and needn't reach their ends.
All inputs are finite; a program needn't handle non-finite values.
Results may differ from the reference program's by a relative error of at most 0.008.
Values sent between devices are 32-bit elements; how exact they have to be, the bound alone decides.
A program may use at most 192 MiB of HBM per device.

```python
import jax
import jax.numpy as jnp

ROOT = 16384
CHILD = 8192
LEAF = 4096
SOURCES = 128


def levels(key, dims, cuts, smallest, high):
    def one(dim, parts):
        heights = jax.random.uniform(jax.random.fold_in(jax.random.fold_in(key, 6), dim), (parts,), jnp.float32, smallest / len(cuts), high / len(cuts))
        return jnp.repeat(jnp.exp(heights), dims[dim] // parts).reshape((-1,) + (1,) * (len(dims) - dim - 1))

    level = one(*cuts[0])
    for cut in cuts[1:]:
        level = level * one(*cut)
    return level


def centred(own_key, extent, width, reach, cuts=(), kind=jnp.bfloat16):
    factor_of = levels(own_key, extent, cuts, -0.22, 0.18) if cuts else 1.0
    drawn = jax.random.normal(own_key, extent, jnp.float32) * width * factor_of
    return jnp.minimum(jnp.maximum(drawn, -reach), reach).astype(kind)


def setup_inputs(seed: int = 0) -> dict:
    arg_keys = jax.random.split(jax.random.key(seed), 10)
    rhs_root = centred(arg_keys[0], (ROOT, SOURCES), 1.0, 6.0, ((0, 4),), jnp.float32)
    rhs_child = centred(arg_keys[1], (2, CHILD, SOURCES), 1.0, 6.0, ((0, 2), (1, 4)), jnp.float32)
    rhs_leaf = centred(arg_keys[2], (4, LEAF, SOURCES), 1.0, 6.0, ((0, 2), (1, 4)), jnp.float32)
    root_inv = centred(arg_keys[3], (ROOT, ROOT), ROOT ** -0.5, 0.046875, ((0, 4), (1, 4)))
    child_inv = centred(arg_keys[4], (2, CHILD, CHILD), CHILD ** -0.5, 0.0625, ((0, 2), (1, 4), (2, 4)))
    leaf_inv = centred(arg_keys[5], (4, LEAF, LEAF), LEAF ** -0.5, 0.09375, ((0, 2), (1, 4), (2, 4)))
    leaf_to_child = centred(arg_keys[6], (4, CHILD, LEAF), (2 * LEAF) ** -0.5, 0.0625, ((0, 2), (1, 4), (2, 4)))
    leaf_to_root = centred(arg_keys[7], (4, ROOT, LEAF), (2 * CHILD + 4 * LEAF) ** -0.5, 0.03125, ((0, 2), (1, 4), (2, 4)))
    child_to_root = centred(arg_keys[8], (2, ROOT, CHILD), (2 * CHILD + 4 * LEAF) ** -0.5, 0.03125, ((0, 2), (1, 4), (2, 4)))
    return dict(rhs_root=rhs_root, rhs_child=rhs_child, rhs_leaf=rhs_leaf, root_inv=root_inv, child_inv=child_inv, leaf_inv=leaf_inv, leaf_to_child=leaf_to_child, leaf_to_root=leaf_to_root, child_to_root=child_to_root)


def mul(matrix, vector):
    return jnp.dot(matrix, vector.astype(jnp.bfloat16), preferred_element_type=jnp.float32)


def reference(rhs_root, rhs_child, rhs_leaf, root_inv, child_inv, leaf_inv, leaf_to_child, leaf_to_root, child_to_root):
    y_leaf = [mul(leaf_inv[g], rhs_leaf[g]) for g in range(4)]
    y_child = []
    for c in range(2):
        r_child = rhs_child[c] - mul(leaf_to_child[2 * c], y_leaf[2 * c]) - mul(leaf_to_child[2 * c + 1], y_leaf[2 * c + 1])
        y_child.append(mul(child_inv[c], r_child))
    r_root = rhs_root
    for c in range(2):
        r_root = r_root - mul(child_to_root[c], y_child[c])
    for g in range(4):
        r_root = r_root - mul(leaf_to_root[g], y_leaf[g])
    y_root = mul(root_inv, r_root)
    x_root = mul(root_inv.T, y_root)
    x_child = []
    for c in range(2):
        v = y_child[c] - mul(child_to_root[c].T, x_root)
        x_child.append(mul(child_inv[c].T, v))
    x_leaf = []
    for g in range(4):
        v = y_leaf[g] - mul(leaf_to_child[g].T, x_child[g // 2]) - mul(leaf_to_root[g].T, x_root)
        x_leaf.append(mul(leaf_inv[g].T, v))
    return x_root, jnp.stack(x_child), jnp.stack(x_leaf), y_root
```

```python
import functools

import jax
import jax.numpy as jnp
from jax import lax
from jax.experimental import pallas as pl
from jax.experimental.pallas import tpu as pltpu
from jax.sharding import PartitionSpec as P

F32 = jnp.float32
CHUNKS = 8


def half16(values):
    return values.astype(jnp.bfloat16)


def remote(src, dst, send, recv, axis, index):
    return pltpu.make_async_remote_copy(
        src_ref=src,
        dst_ref=dst,
        send_sem=send,
        recv_sem=recv,
        device_id={axis: index},
        device_id_type=pl.DeviceIdType.MESH,
    )


def greet(partners):
    barrier = pltpu.get_barrier_semaphore()
    for axis, index in partners:
        pl.semaphore_signal(
            barrier, inc=1, device_id={axis: index}, device_id_type=pl.DeviceIdType.MESH
        )
    pl.semaphore_wait(barrier, len(partners))


def rows_at(start, size):
    return pl.ds(pl.multiple_of(start, 8), size)


def col_kernel(chunks, d, o, x, s, y, t, s0, r0, s1, r1, s2, r2):
    me = lax.axis_index("col")
    core, chip = lax.rem(me, 2), lax.div(me, 2)
    twin, across = 2 * chip + 1 - core, 2 * (1 - chip) + core
    half = d.shape[0] // 2
    size = half // chunks
    greet([("col", twin), ("col", across)])
    first, second, third = [], [], []
    for c in range(chunks):
        at = pl.ds(c * size, size)
        src = d.at[rows_at((1 - core) * half + c * size, size)]
        first.append(remote(src, x.at[at], s0.at[c], r0.at[c], "col", twin))
        first[-1].start()
    for c in range(chunks):
        at = pl.ds(c * size, size)
        first[c].wait_recv()
        s[at] = d[rows_at(core * half + c * size, size)] + x[at]
        second.append(remote(s.at[at], y.at[at], s1.at[c], r1.at[c], "col", across))
        second[-1].start()
    for c in range(chunks):
        at = pl.ds(c * size, size)
        mine = rows_at(core * half + c * size, size)
        second[c].wait_recv()
        t[mine] = s[at] + y[at]
        third.append(remote(t.at[mine], t.at[mine], s2.at[c], r2.at[c], "col", twin))
        third[-1].start()
    for c in range(chunks):
        third[c].wait_recv()
    o[...] = t[...]
    for copy in first + second + third:
        copy.wait_send()


def col_layer_kernel(chunks, d, o, x, u, w, s, y, t, s0, r0, s1, r1, s2, r2, s3, r3, s4, r4):
    me, layer = lax.axis_index("col"), lax.axis_index("layer")
    core, chip = lax.rem(me, 2), lax.div(me, 2)
    twin, across, other = 2 * chip + 1 - core, 2 * (1 - chip) + core, 1 - layer
    half = d.shape[0] // 2
    quarter = half // 2
    size = quarter // chunks
    greet([("col", twin), ("col", across), ("layer", other)])

    def place(core_of, layer_of, c):
        return rows_at(core_of * half + layer_of * quarter + c * size, size)

    cores, layers, chips, backs, gathers = [], [], [], [], []
    for g, part in enumerate((other, layer)):
        for c in range(chunks):
            i = g * chunks + c
            src = d.at[place(1 - core, part, c)]
            cores.append(
                remote(src, x.at[pl.ds(i * size, size)], s0.at[i], r0.at[i], "col", twin)
            )
            cores[-1].start()
    for c in range(chunks):
        at = pl.ds(c * size, size)
        cores[c].wait_recv()
        u[at] = d[place(core, other, c)] + x[at]
        layers.append(remote(u.at[at], w.at[at], s1.at[c], r1.at[c], "layer", other))
        layers[-1].start()
    for c in range(chunks):
        at = pl.ds(c * size, size)
        cores[chunks + c].wait_recv()
        layers[c].wait_recv()
        s[at] = d[place(core, layer, c)] + x[pl.ds((chunks + c) * size, size)] + w[at]
        chips.append(remote(s.at[at], y.at[at], s2.at[c], r2.at[c], "col", across))
        chips[-1].start()
    for c in range(chunks):
        at = pl.ds(c * size, size)
        mine = place(core, layer, c)
        chips[c].wait_recv()
        t[mine] = s[at] + y[at]
        backs.append(remote(t.at[mine], t.at[mine], s3.at[c], r3.at[c], "layer", other))
        backs[-1].start()
        gathers.append(remote(t.at[mine], t.at[mine], s4.at[c], r4.at[c], "col", twin))
        gathers[-1].start()
    for c in range(chunks):
        i = chunks + c
        theirs = place(core, other, c)
        backs[c].wait_recv()
        gathers.append(remote(t.at[theirs], t.at[theirs], s4.at[i], r4.at[i], "col", twin))
        gathers[-1].start()
    for copy in gathers:
        copy.wait_recv()
    o[...] = t[...]
    for copy in cores + layers + chips + backs + gathers:
        copy.wait_send()


def row_kernel(n, chunks, scatter, gather, d, o, acc, ab, w, t, s0, r0, s1, s2, rab, s3, r3):
    me, layer = lax.axis_index("row"), lax.axis_index("layer")
    other = 1 - layer
    left = me < n // 2
    middle = (me == n // 2 - 1) | (me == n // 2)
    inside = (me > 0) & (me < n - 1)
    inner = jnp.where(left, me + 1, me - 1)
    outer = jnp.where(left, jnp.maximum(me - 1, 0), jnp.minimum(me + 1, n - 1))
    slot = jnp.where(middle, 1, 0)
    rows = acc.shape[0]
    size = rows // chunks

    barrier = pltpu.get_barrier_semaphore()

    def signal(axis, index):
        pl.semaphore_signal(
            barrier, inc=1, device_id={axis: index}, device_id_type=pl.DeviceIdType.MESH
        )

    signal("row", inner)
    if scatter or gather:
        signal("layer", other)

    @pl.when(inside)
    def _():
        signal("row", outer)

    peers = 2 if scatter or gather else 1
    pl.semaphore_wait(barrier, peers + jnp.where(inside, 1, 0))

    def at(c):
        return pl.ds(c * size, size)

    def own(c):
        return rows_at(layer * rows + c * size, size) if gather else at(c)

    def swap(c):
        src = d.at[rows_at(other * rows + c * size, size)]
        return remote(src, w.at[at(c)], s0.at[c], r0.at[c], "layer", other)

    def inward(c):
        return remote(
            acc.at[at(c)], ab.at[slot, at(c)], s1.at[c], rab.at[slot, c], "row", inner
        )

    def from_outer(c):
        return remote(acc.at[at(c)], ab.at[0, at(c)], s1.at[c], rab.at[0, c], "row", inner)

    def outward(c):
        return remote(t.at[own(c)], ab.at[1, at(c)], s2.at[c], rab.at[1, c], "row", outer)

    def hand(c):
        return remote(t.at[own(c)], t.at[own(c)], s3.at[c], r3.at[c], "layer", other)

    def first(c, has_outer):
        if scatter:
            swap(c).wait_recv()
            mine = d[rows_at(layer * rows + c * size, size)] + w[at(c)]
        else:
            mine = d[at(c)]
        if has_outer:
            from_outer(c).wait_recv()
            mine = mine + ab[0, at(c)]
        acc[at(c)] = mine
        inward(c).start()

    def second(c, has_outer):
        outward(c).wait_recv()
        arrived = ab[1, at(c)]
        t[own(c)] = jnp.where(middle, acc[at(c)] + arrived, arrived)
        if has_outer:
            outward(c).start()
        if gather:
            hand(c).start()

    if scatter:
        for c in range(chunks):
            swap(c).start()

    @pl.when(inside)
    def _():
        for c in range(chunks + 1):
            if c < chunks:
                first(c, True)
            if c > 0:
                second(c - 1, True)
        for c in range(chunks):
            outward(c).wait_send()

    @pl.when(jnp.logical_not(inside))
    def _():
        for c in range(chunks):
            first(c, False)
        for c in range(chunks):
            second(c, False)

    for c in range(chunks):
        if gather:
            hand(c).wait_recv()
            hand(c).wait_send()
        if scatter:
            swap(c).wait_send()
        inward(c).wait_send()
    o[...] = t[...]


def run(kernel, rows, scratch, ident, values):
    return pl.pallas_call(
        kernel,
        out_shape=jax.ShapeDtypeStruct((rows, values.shape[1]), F32),
        in_specs=[pl.BlockSpec(memory_space=pltpu.VMEM)],
        out_specs=pl.BlockSpec(memory_space=pltpu.VMEM),
        scratch_shapes=scratch,
        compiler_params=pltpu.CompilerParams(
            collective_id=ident, has_side_effects=True, vmem_limit_bytes=24 * 2**20
        ),
    )(values)


def col_sum(values, ident):
    flat = values.reshape(-1, values.shape[-1])
    rows, wide = flat.shape
    sems = [pltpu.SemaphoreType.DMA((CHUNKS,))] * 6
    half = pltpu.VMEM((rows // 2, wide), F32)
    scratch = [half, half, half, pltpu.VMEM((rows, wide), F32)] + sems
    out = run(functools.partial(col_kernel, CHUNKS), rows, scratch, ident, flat)
    return out.reshape(values.shape)


def col_layer_sum(values, ident):
    rows, wide = values.shape
    one, two = pltpu.SemaphoreType.DMA((CHUNKS,)), pltpu.SemaphoreType.DMA((2 * CHUNKS,))
    quarter = pltpu.VMEM((rows // 4, wide), F32)
    scratch = [pltpu.VMEM((rows // 2, wide), F32)] + [quarter] * 4
    scratch += [pltpu.VMEM((rows, wide), F32), two, two] + [one] * 6 + [two, two]
    return run(functools.partial(col_layer_kernel, CHUNKS), rows, scratch, ident, values)


def row_sum(n, values, ident, scatter=False, gather=False):
    flat = values.reshape(-1, values.shape[-1])
    rows, wide = flat.shape
    if scatter:
        rows = rows // 2
    total = 2 * rows if gather else rows
    one = pltpu.SemaphoreType.DMA((CHUNKS,))
    scratch = [
        pltpu.VMEM((rows, wide), F32),
        pltpu.VMEM((2, rows, wide), F32),
        pltpu.VMEM((rows if scatter else 8, wide), F32),
        pltpu.VMEM((total, wide), F32),
        one,
        one,
        one,
        one,
        pltpu.SemaphoreType.DMA((2, CHUNKS)),
        one,
        one,
    ]
    kernel = functools.partial(row_kernel, n, CHUNKS, scatter, gather)
    out = run(kernel, total, scratch, ident, flat)
    return out if scatter or gather else out.reshape(values.shape)


def on_device(
    n,
    rhs_root,
    rhs_child,
    rhs_leaf,
    root_inv,
    child_inv,
    leaf_inv,
    leaf_to_child,
    leaf_to_root,
    child_to_root,
):
    layer = lax.axis_index("layer")
    wide = rhs_root.shape[0] // 2
    rhs_half = lax.dynamic_slice_in_dim(rhs_root, layer * wide, wide, 0)
    root_half = lax.dynamic_slice_in_dim(root_inv, layer * wide, wide, 1)

    y_leaf = col_sum(
        jnp.einsum("gij,gjs->gis", leaf_inv, half16(rhs_leaf), preferred_element_type=F32), 0
    )
    leaf_bf = half16(y_leaf)
    leaf_update = jnp.einsum("gij,gjs->is", leaf_to_root, leaf_bf, preferred_element_type=F32)
    r_child = rhs_child[0] - row_sum(
        n, jnp.einsum("gij,gjs->is", leaf_to_child, leaf_bf, preferred_element_type=F32), 1
    )
    y_child = col_sum(jnp.dot(child_inv[0], half16(r_child), preferred_element_type=F32), 2)
    child_update = jnp.dot(child_to_root[0], half16(y_child), preferred_element_type=F32)
    r_root = rhs_half - row_sum(n, child_update + leaf_update, 3, scatter=True)
    y_root = col_layer_sum(jnp.dot(root_half, half16(r_root), preferred_element_type=F32), 4)
    x_root = row_sum(
        n,
        jnp.einsum("ij,is->js", root_half, half16(y_root), preferred_element_type=F32),
        5,
        gather=True,
    )
    root_bf = half16(x_root)
    back_child = y_child - col_sum(
        jnp.einsum("ij,is->js", child_to_root[0], root_bf, preferred_element_type=F32), 6
    )
    x_child = row_sum(
        n,
        jnp.einsum("ij,is->js", child_inv[0], half16(back_child), preferred_element_type=F32),
        7,
    )
    terms = jnp.einsum("gij,is->gjs", leaf_to_child, half16(x_child), preferred_element_type=F32)
    terms = terms + jnp.einsum("gij,is->gjs", leaf_to_root, root_bf, preferred_element_type=F32)
    back_leaf = y_leaf - col_sum(terms, 8)
    x_leaf = row_sum(
        n,
        jnp.einsum("gij,gis->gjs", leaf_inv, half16(back_leaf), preferred_element_type=F32),
        9,
    )
    return (x_root, x_child[None], x_leaf, y_root)


def solution(mesh):
    in_specs = (
        P("col", None),
        P("layer", "col", None),
        P("layer", "col", None),
        P("row", "col"),
        P("layer", "row", "col"),
        P("layer", "row", "col"),
        P("layer", "col", "row"),
        P("layer", "col", "row"),
        P("layer", "col", "row"),
    )
    out_specs = (P("col", None), P("layer", "col", None), P("layer", "col", None), P("row", None))
    return jax.shard_map(
        functools.partial(on_device, mesh.shape["row"]),
        mesh=mesh,
        in_specs=in_specs,
        out_specs=out_specs,
        check_vma=False,
    )
```
